32 devices in a mesh: layer: 2 (over core), expert: 4 (over y, x), matrix: 4 (over z).
Axes of the slice: x: 2, y: 2, z: 4, core: 2. Of those that a mesh axis runs over, the one named last changes fastest.
Arguments:
- grads: float32 [8, 1, 2048, 768], P(('layer', 'expert'), None, 'matrix'), parts along dimension 0, may hold values from -6 to 6
- basis_out: float32 [8, 2048, 2048], P('layer', None, ('expert', 'matrix')), parts along dimension 0, may hold values from -0.125 to 0.125
- basis_in: float32 [8, 768, 768], P('layer', ('expert', 'matrix')), parts along dimension 0, may hold values from -0.21875 to 0.21875
- eigvals: float32 [8, 2048, 768], P('layer', ('expert', 'matrix')), parts along dimension 0, may hold values from 0.001 to 1
- counts: int32 [8], P(('layer', 'expert')), parts along dimension 0, may hold values from 0 to 1, as said below
- slot_query: int32 [8, 1], P(('layer', 'expert')), parts along dimension 0, may hold values from 0 to 31
Outputs:
- precond: float32 [8, 1, 2048, 768], P(('layer', 'expert'), None, 'matrix'), parts along dimension 0
- scores: float32 [64], P('layer'), parts along dimension 0
The draws below stay inside these ranges and needn't reach their ends.
There are 2 independent parts, one for each index of `layer`. The reference program is written for one: setup_inputs(seed, part) draws one part's arguments, and reference() takes and returns one part's arrays. A program takes and returns all parts, laid end to end along the dimension named above; each array names one. Nothing has to cross between parts.
Inputs may be any that keep to these rules, and one draw needn't show every extreme that they name: `counts`: some expert has no live slot and some expert has all 1.
All inputs are finite; a program needn't handle non-finite values.
Results may differ from the reference program's by a relative error of at most 0.0003.
Values sent between devices are 32-bit elements; how exact they have to be, the bound alone decides.
No kernel may reach another device: no remote copies, remote signals or barrier semaphores. Data moves between devices by JAX's collectives and lax.ppermute only.
A program may use at most 64 MiB of HBM per device.

```python
import math
import jax
import jax.numpy as jnp
from jax import lax

D = 2048
F = 768
CAP = 1
QUERIES = 32
EXPERTS = 4


def draw_counts(key, part):
    base = jax.random.randint(key, (EXPERTS,), 0, CAP + 1)
    chosen = jax.random.randint(jax.random.fold_in(key, 7), (), 0, EXPERTS)
    offset = jax.random.randint(jax.random.fold_in(key, 11), (), 1, EXPERTS)
    emptied = (chosen + offset) % EXPERTS
    where = jnp.arange(EXPERTS)
    filled = jnp.where(where == chosen, CAP, base)
    return jnp.where(where == emptied, 0, filled).astype(jnp.int32)


def plant(values, stream_key, least, top_value):
    shape = values.shape
    place = [jax.random.randint(jax.random.fold_in(stream_key, axis), (), 0, shape[axis]) for axis in range(len(shape))]
    values = values.at[tuple(place)].set(least)
    longest = shape.index(max(shape))
    place[longest] = (place[longest] + 1) % shape[longest]
    return values.at[tuple(place)].set(top_value)


def level_of(stream_key, dims, shards, low, largest):
    def one(axis_at, parts):
        steps = jax.random.uniform(jax.random.fold_in(jax.random.fold_in(stream_key, 6), axis_at), (parts,), jnp.float32, low / len(shards), largest / len(shards))
        return jnp.repeat(jnp.exp(steps), dims[axis_at] // parts).reshape((-1,) + (1,) * (len(dims) - axis_at - 1))

    level = one(*shards[0])
    for cut in shards[1:]:
        level = level * one(*cut)
    return level


def scatter_about(own_key, dims, spread, most, shards=(), held_as=jnp.bfloat16):
    values = spread * jax.random.normal(own_key, dims, jnp.float32)
    if shards:
        values = values * level_of(own_key, dims, shards, -0.22, 0.18)
    return jnp.clip(values, -most, most).astype(held_as)


def setup_inputs(seed: int = 0, part: int = 0) -> dict:
    arg_keys = jax.random.split(jax.random.key(seed), 7)
    own_keys = jax.random.split(jax.random.fold_in(arg_keys[6], part), 7)
    grads = scatter_about(own_keys[0], (EXPERTS, CAP, D, F), 1.0, 6.0, ((0, 4), (2, 4)), jnp.float32)
    basis_out = scatter_about(own_keys[1], (EXPERTS, D, D), D ** -0.5, 0.125, ((2, 16),), jnp.float32)
    basis_in = scatter_about(own_keys[2], (EXPERTS, F, F), F ** -0.5, 0.21875, ((1, 16),), jnp.float32)
    eigvals = jnp.clip(jnp.exp(math.log(1.0) - 6.9077552 * jax.random.uniform(own_keys[3], (EXPERTS, D, F), jnp.float32) ** level_of(own_keys[3], (EXPERTS, D, F), ((1, 16),), -0.2, 0.2)), 0.001, 1.0)
    counts = draw_counts(jax.random.fold_in(jax.random.fold_in(arg_keys[6], part), 71), part)
    slot_query = plant(jax.random.randint(own_keys[5], (EXPERTS, CAP), 0, QUERIES), jax.random.fold_in(own_keys[5], 1), 0, QUERIES - 1).astype(jnp.int32)
    return {"grads": grads, "basis_out": basis_out, "basis_in": basis_in, "eigvals": eigvals, "counts": counts, "slot_query": slot_query}


damping_fixed = 0.05
highest = lax.Precision.HIGHEST


def one_expert(items):
    grads_e, basis_out_e, basis_in_e, eigvals_e, count_e, queries_e = items
    outputs = []
    contrib = jnp.zeros((QUERIES,), jnp.float32)
    targets = jnp.arange(QUERIES, dtype=jnp.int32)
    for slot_index in range(CAP):
        gradient = grads_e[slot_index]
        rotated = jnp.dot(jnp.dot(basis_out_e.T, gradient, precision=highest), basis_in_e, precision=highest)
        scaled = rotated / (eigvals_e + damping_fixed)
        back = jnp.dot(scaled, basis_in_e.T, precision=highest)
        result = jnp.dot(basis_out_e, back, precision=highest)
        live = (slot_index < count_e).astype(jnp.float32)
        result = result * live
        outputs.append(result)
        value = jnp.sum(gradient * result) / (D * F)
        onehot = (queries_e[slot_index] == targets).astype(jnp.float32)
        contrib = contrib + value * onehot
    return jnp.stack(outputs), contrib


def reference(grads, basis_out, basis_in, eigvals, counts, slot_query):
    precond, contribs = lax.map(one_expert, (grads, basis_out, basis_in, eigvals, counts, slot_query))
    scores = jnp.sum(contribs, axis=0)
    return precond, scores
```

```python
import functools

import jax
import jax.numpy as jnp
from jax import lax
from jax.experimental import pallas as pl
from jax.experimental.pallas import tpu as pltpu
from jax.sharding import PartitionSpec as P

QUERIES = 32

damping_fixed = 0.05
F32 = jnp.float32
BF16 = jnp.bfloat16

IDLE, ONE_BLOCK, TWO_BLOCKS = 0, 1, 2


def split(x):
    high = x.astype(BF16)
    return high, (x - high.astype(F32)).astype(BF16)


def three_pass(a, b, contract):
    dims = (contract, ((), ()))
    dot = functools.partial(lax.dot_general, dimension_numbers=dims, preferred_element_type=F32)
    return dot(a[0], b[0]) + (dot(a[0], b[1]) + dot(a[1], b[0]))


def pack_kernel(experts, meta, outs, eigs, *refs):
    packed, sems = refs[:experts], refs[experts]
    depth, width = outs.shape[1], outs.shape[2]
    height = eigs.shape[1]
    chunks = eigs.shape[2] // width
    copies = []
    for distance in range(experts):
        target = lax.bitwise_xor(meta[2], distance)
        base = distance * (chunks + 1)
        copies.append(
            pltpu.make_async_copy(outs.at[target], packed[distance].at[pl.ds(0, depth), :], sems.at[base])
        )
        for chunk in range(chunks):
            copies.append(
                pltpu.make_async_copy(
                    eigs.at[target, :, pl.ds(chunk * width, width)],
                    packed[distance].at[pl.ds(depth + chunk * height, height), :],
                    sems.at[base + 1 + chunk],
                )
            )
    for copy in copies:
        copy.start()
    for copy in copies:
        copy.wait()


def pack(meta, outs, eigs):
    experts, depth, width = outs.shape
    chunks = eigs.shape[2] // width
    in_hbm = pl.BlockSpec(memory_space=pltpu.HBM)
    shape = jax.ShapeDtypeStruct((depth + chunks * eigs.shape[1], width), F32)
    return pl.pallas_call(
        functools.partial(pack_kernel, experts),
        out_shape=[shape] * experts,
        in_specs=[pl.BlockSpec(memory_space=pltpu.SMEM), in_hbm, in_hbm],
        out_specs=[pl.BlockSpec(memory_space=pltpu.VMEM)] * experts,
        scratch_shapes=[pltpu.SemaphoreType.DMA((experts * (chunks + 1),))],
        compiler_params=pltpu.CompilerParams(vmem_limit_bytes=32 * 1024 * 1024),
        cost_estimate=pl.CostEstimate(flops=0, bytes_accessed=8 * (outs.size + eigs.size), transcendentals=0),
        name="pack",
    )(meta, outs, eigs)


def block_kernel(planes, inner_job, second, n_own, n_piece, fused, meta, *refs):
    refs = list(refs)

    def take(number):
        taken, refs[:number] = refs[:number], []
        return taken

    hops = planes - 1
    here_refs = take(2 if fused else 1)
    near_up, near_down = take(2 if fused else 1), take(2 if fused else 1)
    far_up, far_down = take(hops - 1), take(hops - 1)
    own_refs, piece_refs = take(n_own), take(n_piece)
    in_refs = take(0 if fused else 1)
    earlier = take(2 * planes - 1) if second else None
    sums = take(2 * planes - 1)
    (energy,) = take(1)
    grad, cols, cols_high, cols_low, eig, inner, work, rotated, back_high, back_low, total = take(11)
    out_sems, eig_sems, grad_sems, in_sems, sum_sems = refs
    rows = grad.shape[1]
    here, role, expert, live = meta[0], meta[1], meta[2], meta[3]
    depth, block = cols.shape

    def relative(target, plane):
        if target < plane:
            return plane - target
        if target > plane:
            return hops + target - plane
        return 0

    def per_plane(action):
        for plane in range(planes):
            pl.when(here == plane)(functools.partial(action, plane))

    def per_plane_and_role(action):
        if not second:
            for plane in range(planes):
                pl.when((here == plane) & (role == ONE_BLOCK))(functools.partial(action, plane, False))
        if inner_job:
            for plane in (1, planes - 2):
                pl.when((here == plane) & (role == TWO_BLOCKS))(functools.partial(action, plane, True))

    def sources(target, plane, inner_only):
        distance = abs(target - plane)
        if distance == 0:
            return here_refs
        if distance == 1:
            return near_up if target < plane else near_down
        step = hops if inner_only else distance
        ref = (far_up if target < plane else far_down)[step - 2]
        if not fused:
            return [ref]
        return [ref.at[pl.ds(0, rows), :], ref.at[pl.ds(rows, ref.shape[0] - rows), :]]

    def compute():
        pieces = n_piece + (1 if n_own else 0)
        width = height = block // pieces
        out_copies, eig_copies = [], []

        def place(copies, sems, source, spot):
            copies.append(pltpu.make_async_copy(source, spot, sems.at[len(copies)]))

        owns = [ref.at[expert] if len(ref.shape) == 3 else ref for ref in own_refs]
        first = 1 if n_own else 0
        if n_own:
            place(out_copies, out_sems, owns[0], cols.at[:, pl.ds(0, width)])
            place(eig_copies, eig_sems, owns[1], eig.at[pl.ds(0, height), :])
        for index, ref in enumerate(piece_refs, first):
            place(out_copies, out_sems, ref.at[pl.ds(0, depth), :], cols.at[:, pl.ds(index * width, width)])
            for chunk in range(eig.shape[1] // width):
                spot = eig.at[pl.ds(index * height, height), pl.ds(chunk * width, width)]
                place(eig_copies, eig_sems, ref.at[pl.ds(depth + chunk * height, height), :], spot)
        for copy in out_copies:
            copy.start()

        in_copies = []

        def in_copy(target, distance, source):
            part = source.shape[0] // pieces
            owner = lax.bitwise_xor(expert, distance)
            to = pl.multiple_of((owner * planes + target) * part, part)
            window = source.at[pl.ds(distance * part, part), :]
            sem = in_sems.at[target * pieces + distance]
            return pltpu.make_async_copy(window, inner.at[pl.ds(to, part), :], sem)

        def start_shards(plane, inner_only):
            for target in range(planes):
                source = sources(target, plane, inner_only)[0]
                pltpu.make_async_copy(source, grad.at[target], grad_sems.at[target]).start()
            if fused:
                for target in range(planes):
                    source = sources(target, plane, inner_only)[1]
                    for distance in range(pieces):
                        in_copy(target, distance, source).start()

        per_plane_and_role(start_shards)
        if fused:
            in_copies += [in_copy(t, d, here_refs[1]) for t in range(planes) for d in range(pieces)]
        else:
            in_copies.append(pltpu.make_async_copy(in_refs[0], inner, in_sems.at[0]))
            in_copies[0].start()
        for copy in eig_copies:
            copy.start()
        if second:

            def start_earlier(plane):
                for target in range(planes):
                    source = earlier[relative(target, plane)]
                    pltpu.make_async_copy(source, total.at[target], sum_sems.at[target]).start()

            per_plane(start_earlier)

        for copy in out_copies:
            copy.wait()
        work[...] = jnp.zeros_like(work)

        @pl.loop(0, planes)
        def _(target):
            pltpu.make_async_copy(here_refs[0], grad.at[target], grad_sems.at[target]).wait()
            window = pl.ds(pl.multiple_of(target * rows, rows), rows)
            left = split(cols[window, :])
            cols_high[window, :] = left[0]
            cols_low[window, :] = left[1]
            work[...] += three_pass(left, split(grad[target]), ((0,), (0,)))

        for copy in in_copies:
            copy.wait()
        rotated[...] = three_pass(split(work[...]), split(inner[...]), ((1,), (0,)))
        for copy in eig_copies:
            copy.wait()
        alive = (live > 0).astype(F32)
        turned = rotated[...]
        scaled = turned / (eig[...] + damping_fixed) * alive
        work[...] = scaled
        energy[...] = jnp.sum(turned * scaled, axis=0, keepdims=True)
        high, low = split(three_pass(split(work[...]), split(inner[...]), ((1,), (1,))))
        back_high[...] = high
        back_low[...] = low

        def out_copy(target, plane):
            return pltpu.make_async_copy(
                total.at[target], sums[relative(target, plane)], sum_sems.at[planes + target]
            )

        for target in range(planes):
            window = pl.ds(target * rows, rows)
            product = three_pass(
                (cols_high[window, :], cols_low[window, :]), (back_high[...], back_low[...]), ((1,), (0,))
            )
            if second:
                pltpu.make_async_copy(earlier[0], total.at[target], sum_sems.at[target]).wait()
                total[target] += product
            else:
                total[target] = product
            per_plane(lambda plane, target=target: out_copy(target, plane).start())
        for target in range(planes):
            out_copy(target, target).wait()

    def idle():
        energy[...] = jnp.zeros_like(energy)
        if not second:
            total[0] = jnp.zeros_like(total[0])
            copy = pltpu.make_async_copy(total.at[0], sums[0], sum_sems.at[0])
            copy.start()
            copy.wait()

    least = TWO_BLOCKS if second else ONE_BLOCK
    pl.when(role >= least)(compute)
    pl.when(role < least)(idle)


def run_block(planes, block, inner_job, meta, shards, owns, pieces, inners, earlier=None):
    second = earlier is not None
    rows, width = shards[0].shape
    operands = [*shards, *owns, *pieces, *inners, *(earlier or [])]
    in_hbm = pl.BlockSpec(memory_space=pltpu.HBM)
    sums = [jax.ShapeDtypeStruct((rows, width), F32)] * (2 * planes - 1)
    first_alias = 1 + len(operands) - len(sums)
    number = len(pieces) + (1 if owns else 0)
    dma = pltpu.SemaphoreType.DMA
    flops = 2 * block * width * (2 * rows * planes + 2 * width)
    results = pl.pallas_call(
        functools.partial(block_kernel, planes, inner_job, second, len(owns), len(pieces), not inners),
        out_shape=[*sums, jax.ShapeDtypeStruct((1, width), F32)],
        in_specs=[pl.BlockSpec(memory_space=pltpu.SMEM)] + [in_hbm] * len(operands),
        out_specs=[in_hbm] * len(sums) + [pl.BlockSpec(memory_space=pltpu.VMEM)],
        scratch_shapes=[
            pltpu.VMEM((planes, rows, width), F32),
            pltpu.VMEM((planes * rows, block), F32),
            pltpu.VMEM((planes * rows, block), BF16),
            pltpu.VMEM((planes * rows, block), BF16),
            pltpu.VMEM((block, width), F32),
            pltpu.VMEM((width, width), F32),
            pltpu.VMEM((block, width), F32),
            pltpu.VMEM((block, width), F32),
            pltpu.VMEM((block, width), BF16),
            pltpu.VMEM((block, width), BF16),
            pltpu.VMEM((planes, rows, width), F32),
            dma((number,)),
            dma((1 + number * max(1, width * number // block),)),
            dma((planes,)),
            dma((planes * number,)),
            dma((2 * planes,)),
        ],
        input_output_aliases={first_alias + i: i for i in range(len(sums))} if second else {},
        cost_estimate=pl.CostEstimate(flops=3 * flops, bytes_accessed=4 * 5 * rows * planes * width, transcendentals=0),
        compiler_params=pltpu.CompilerParams(vmem_limit_bytes=56 * 1024 * 1024),
        name="second_block" if second else "first_block",
    )(meta, *operands)
    return results[:-1], results[-1]


def shards(grads, basis_out, basis_in, eigvals, counts, slot_query):
    experts = lax.axis_size("expert")
    planes = lax.axis_size("matrix")
    layers = lax.axis_size("layer")
    expert = lax.axis_index("expert")
    here = lax.axis_index("matrix")
    layer = lax.axis_index("layer")
    rows, width = grads.shape[2], grads.shape[3]
    depth = rows * planes
    last = planes - 1
    inward = [l == 0 and layers == 2 and planes == 4 for l in range(layers)]

    takes_over = jnp.asarray(inward)[layer]
    at_end = (here == 0) | (here == last)
    role = jnp.where(takes_over, jnp.where(at_end, IDLE, TWO_BLOCKS), ONE_BLOCK)
    meta = jnp.stack([here, role, expert, counts[0]]).astype(jnp.int32)

    def move(x, pairs):
        return lax.ppermute(x, ("layer", "matrix"), [(l * planes + a, l * planes + b) for l, a, b in pairs])

    def mirror(pairs):
        return [(l, last - a, last - b) for l, a, b in pairs]

    def gather_pairs(step):
        pairs = [(l, a, a + 1) for l in range(layers) if not inward[l] for a in range(step - 1, last)]
        if step == 1:
            pairs += [(l, a, a + 1) for l in range(layers) if inward[l] for a in range(last - 1)]
        if step == last:
            pairs += [(l, 1, last - 1) for l in range(layers) if inward[l]]
        return pairs

    def reduce_pairs(step):
        low = [1 if inward[l] else 0 for l in range(layers)]
        return [(l, a, a + 1) for l in range(layers) for a in range(low[l], step)]

    def token(x, y):
        mark = x[:8, :128] + y[:8, :128]
        return lax.ppermute(mark, ("layer", "matrix"), [(planes + m, m) for m in range(planes)])

    def near(x):
        return move(x, gather_pairs(1)), move(x, mirror(gather_pairs(1)))

    def far(below, above, ties):
        ups, downs = [below], [above]
        for step in range(2, planes):
            up, down = ups[-1], downs[-1]
            before = list(ties.get(step, ()))
            if any(inward) and step == last:
                before.append(token(up, down))
                up = jnp.where(takes_over, below, up)
                down = jnp.where(takes_over, above, down)
            (up, down), _ = lax.optimization_barrier(((up, down), before))
            ups.append(move(up, gather_pairs(step)))
            downs.append(move(down, mirror(gather_pairs(step))))
        return ups[1:], downs[1:]

    columns, heights = basis_out.shape[2], eigvals.shape[1]
    block = experts * columns
    fits = columns % 128 == 0 and width % columns == 0 and columns == heights
    fits = fits and basis_in.shape[1] % 8 == 0 and experts & (experts - 1) == 0

    def index(l, e, m):
        return (l * experts + e) * planes + m

    def goes_over(l, m):
        return inward[l] and m in (0, last)

    def crossing(x, distance, chosen, turn=lambda m: m):
        every = [(l, e, m) for l in range(layers) for e in range(experts) for m in range(planes)]
        pairs = [(index(l, e, m), index(l, e ^ distance, turn(m))) for l, e, m in every if chosen(l, m)]
        return lax.ppermute(x, ("layer", "expert", "matrix"), pairs)

    own = grads[0, 0]
    own_up, own_down = near(own)
    if fits:
        parts = [
            lax.dynamic_index_in_dim(basis_in, lax.bitwise_xor(expert, distance), 0, keepdims=False)
            for distance in range(experts)
        ]
        parts = [x if d == 0 else crossing(x, d, lambda l, m: True) for d, x in enumerate(parts)]
        packed = pack(meta, basis_out, eigvals)
        parts, packed = lax.optimization_barrier((parts, packed))
        pieces = [crossing(packed[d], d, lambda l, m: not goes_over(l, m)) for d in range(1, experts)]
        over = []
        if any(inward):
            packed, _ = lax.optimization_barrier((packed, (own_up, own_down)))
            over = [crossing(packed[d], d, goes_over, lambda m: 1 if m == 0 else last - 1) for d in range(experts)]
        part = jnp.concatenate(parts)
        part_up, part_down = near(part)
        ties = {2: pieces[:-1], 3: [*pieces[-1:], *over[:1]]}
        below, above = far(jnp.concatenate([own_up, part_up]), jnp.concatenate([own_down, part_down]), ties)
        near_shards = [own, part, own_up, part_up, own_down, part_down]
        first_owns, first_pieces, inners = [basis_out, eigvals], pieces, []
    else:
        eig = lax.all_to_all(eigvals, "expert", split_axis=0, concat_axis=1, tiled=True)[0]
        out = lax.all_to_all(basis_out, "expert", split_axis=0, concat_axis=2, tiled=True)[0]
        inner = lax.all_gather(basis_in, "matrix", axis=1, tiled=True)
        inner = lax.all_to_all(inner, "expert", split_axis=0, concat_axis=0, tiled=True).reshape(width, width)
        below, above = far(own_up, own_down, {})
        near_shards = [own, own_up, own_down]
        first_owns, first_pieces, inners = [out, eig], [], [inner]

    shards_of_job = [*near_shards, *below, *above]
    sums, energy = run_block(planes, block, any(inward), meta, shards_of_job, first_owns, first_pieces, inners)
    if any(inward):
        second_owns, second_pieces = [], []
        if fits:
            second_pieces = over
        else:
            ends = [pair for l in range(layers) if inward[l] for pair in ((l, 0, 1), (l, last, last - 1))]
            second_owns = [move(x, ends) for x in first_owns]
        sums, more = run_block(
            planes, block, True, meta, shards_of_job, second_owns, second_pieces, inners, sums
        )
        energy = energy + more

    below, above = sums[1:planes], sums[planes:]

    def spread(partials, turn):
        moved = None
        for step in range(1, planes):
            partial = partials[last - step]
            moved = move(partial if moved is None else partial + moved, turn(reduce_pairs(step)))
        return moved

    result = sums[0] + (spread(above, lambda pairs: pairs) + spread(below, mirror))

    value = jnp.sum(energy) / (depth * width)
    scores = jnp.where(jnp.arange(QUERIES, dtype=jnp.int32) == slot_query[0, 0], value, 0.0)
    for axis, size in (("expert", experts), ("matrix", planes)):
        if size & (size - 1):
            scores = lax.psum(scores, axis)
            continue
        distance = 1
        while distance < size:
            scores = scores + lax.ppermute(scores, axis, [(i, i ^ distance) for i in range(size)])
            distance *= 2
    return (result[None, None], scores)


def solution(mesh):
    in_specs = (
        P(("layer", "expert"), None, "matrix", None),
        P("layer", None, ("expert", "matrix")),
        P("layer", ("expert", "matrix"), None),
        P("layer", ("expert", "matrix"), None),
        P(("layer", "expert")),
        P(("layer", "expert"), None),
    )
    out_specs = (P(("layer", "expert"), None, "matrix", None), P("layer"))
    return jax.shard_map(shards, mesh=mesh, in_specs=in_specs, out_specs=out_specs, check_vma=False)
```

```python
import functools

import jax
import jax.numpy as jnp
from jax import lax
from jax.experimental import pallas as pl
from jax.experimental.pallas import tpu as pltpu
from jax.sharding import PartitionSpec as P

QUERIES = 32

damping_fixed = 0.05
F32 = jnp.float32
BF16 = jnp.bfloat16

IDLE, ONE_BLOCK, TWO_BLOCKS = 0, 1, 2


def split(x):
    high = x.astype(BF16)
    return high, (x - high.astype(F32)).astype(BF16)


def three_pass(a, b, contract):
    dims = (contract, ((), ()))
    dot = functools.partial(lax.dot_general, dimension_numbers=dims, preferred_element_type=F32)
    return dot(a[0], b[0]) + (dot(a[0], b[1]) + dot(a[1], b[0]))


def pack_kernel(experts, meta, outs, eigs, *refs):
    packed, sems = refs[:experts], refs[experts]
    depth, width = outs.shape[1], outs.shape[2]
    height = eigs.shape[1]
    chunks = eigs.shape[2] // width
    copies = []
    for distance in range(experts):
        target = lax.bitwise_xor(meta[2], distance)
        base = distance * (chunks + 1)
        copies.append(
            pltpu.make_async_copy(outs.at[target], packed[distance].at[pl.ds(0, depth), :], sems.at[base])
        )
        for chunk in range(chunks):
            copies.append(
                pltpu.make_async_copy(
                    eigs.at[target, :, pl.ds(chunk * width, width)],
                    packed[distance].at[pl.ds(depth + chunk * height, height), :],
                    sems.at[base + 1 + chunk],
                )
            )
    for copy in copies:
        copy.start()
    for copy in copies:
        copy.wait()


def pack(meta, outs, eigs):
    experts, depth, width = outs.shape
    chunks = eigs.shape[2] // width
    in_hbm = pl.BlockSpec(memory_space=pltpu.HBM)
    shape = jax.ShapeDtypeStruct((depth + chunks * eigs.shape[1], width), F32)
    return pl.pallas_call(
        functools.partial(pack_kernel, experts),
        out_shape=[shape] * experts,
        in_specs=[pl.BlockSpec(memory_space=pltpu.SMEM), in_hbm, in_hbm],
        out_specs=[pl.BlockSpec(memory_space=pltpu.VMEM)] * experts,
        scratch_shapes=[pltpu.SemaphoreType.DMA((experts * (chunks + 1),))],
        compiler_params=pltpu.CompilerParams(vmem_limit_bytes=32 * 1024 * 1024),
        cost_estimate=pl.CostEstimate(flops=0, bytes_accessed=8 * (outs.size + eigs.size), transcendentals=0),
        name="pack",
    )(meta, outs, eigs)


def join_kernel(refs_in, groups, *refs):
    sources, outs, sems = refs[1 : 1 + refs_in], refs[1 + refs_in : -1], refs[-1]
    copies = []
    at = 0
    for out, number in zip(outs, groups):
        first = 0
        for source in sources[at : at + number]:
            height = source.shape[0]
            copies.append(pltpu.make_async_copy(source, out.at[pl.ds(first, height), :], sems.at[len(copies)]))
            first += height
        at += number
    for copy in copies:
        copy.start()
    for copy in copies:
        copy.wait()


def join(groups, after):
    sources = [x for group in groups for x in group]
    in_hbm = pl.BlockSpec(memory_space=pltpu.HBM)
    shapes = [jax.ShapeDtypeStruct((sum(x.shape[0] for x in group), group[0].shape[1]), F32) for group in groups]
    return pl.pallas_call(
        functools.partial(join_kernel, len(sources), [len(group) for group in groups]),
        out_shape=shapes,
        in_specs=[in_hbm] * (1 + len(sources)),
        out_specs=[pl.BlockSpec(memory_space=pltpu.VMEM)] * len(shapes),
        scratch_shapes=[pltpu.SemaphoreType.DMA((len(sources),))],
        cost_estimate=pl.CostEstimate(flops=0, bytes_accessed=8 * sum(x.size for x in sources), transcendentals=0),
        compiler_params=pltpu.CompilerParams(vmem_limit_bytes=32 * 1024 * 1024),
        name="join",
    )(after, *sources)


def block_kernel(planes, inner_job, second, n_own, n_piece, fused, meta, *refs):
    refs = list(refs)

    def take(number):
        taken, refs[:number] = refs[:number], []
        return taken

    hops = planes - 1
    here_refs = take(2 if fused else 1)
    up_refs, down_refs = take(hops), take(hops)
    own_refs, piece_refs = take(n_own), take(n_piece)
    in_refs = take(0 if fused else 1)
    earlier = take(2 * planes - 1) if second else None
    sums = take(2 * planes - 1)
    (energy,) = take(1)
    grad, cols, cols_high, cols_low, eig, inner, work, rotated, back_high, back_low, total = take(11)
    out_sems, eig_sems, grad_sems, in_sems, sum_sems = refs
    rows = grad.shape[1]
    here, role, expert, live = meta[0], meta[1], meta[2], meta[3]
    depth, block = cols.shape

    def relative(target, plane):
        if target < plane:
            return plane - target
        if target > plane:
            return hops + target - plane
        return 0

    def per_plane(action):
        for plane in range(planes):
            pl.when(here == plane)(functools.partial(action, plane))

    def per_plane_and_role(action):
        if not second:
            for plane in range(planes):
                pl.when((here == plane) & (role == ONE_BLOCK))(functools.partial(action, plane, False))
        if inner_job:
            for plane in (1, planes - 2):
                pl.when((here == plane) & (role == TWO_BLOCKS))(functools.partial(action, plane, True))

    def sources(target, plane, inner_only):
        distance = abs(target - plane)
        if distance == 0:
            return here_refs
        step = hops if inner_only and distance > 1 else distance
        ref = (up_refs if target < plane else down_refs)[step - 1]
        if not fused:
            return [ref]
        return [ref.at[pl.ds(0, rows), :], ref.at[pl.ds(rows, ref.shape[0] - rows), :]]

    def compute():
        pieces = n_piece + (1 if n_own else 0)
        width = height = block // pieces
        out_copies, eig_copies = [], []

        def place(copies, sems, source, spot):
            copies.append(pltpu.make_async_copy(source, spot, sems.at[len(copies)]))

        owns = [ref.at[expert] if len(ref.shape) == 3 else ref for ref in own_refs]
        first = 1 if n_own else 0
        if n_own:
            place(out_copies, out_sems, owns[0], cols.at[:, pl.ds(0, width)])
            place(eig_copies, eig_sems, owns[1], eig.at[pl.ds(0, height), :])
        for index, ref in enumerate(piece_refs, first):
            place(out_copies, out_sems, ref.at[pl.ds(0, depth), :], cols.at[:, pl.ds(index * width, width)])
            for chunk in range(eig.shape[1] // width):
                spot = eig.at[pl.ds(index * height, height), pl.ds(chunk * width, width)]
                place(eig_copies, eig_sems, ref.at[pl.ds(depth + chunk * height, height), :], spot)
        for copy in out_copies:
            copy.start()

        in_copies = []

        def in_copy(target, distance, source):
            part = source.shape[0] // pieces
            owner = lax.bitwise_xor(expert, distance)
            to = pl.multiple_of((owner * planes + target) * part, part)
            window = source.at[pl.ds(distance * part, part), :]
            sem = in_sems.at[target * pieces + distance]
            return pltpu.make_async_copy(window, inner.at[pl.ds(to, part), :], sem)

        def start_shards(plane, inner_only):
            for target in range(planes):
                source = sources(target, plane, inner_only)[0]
                pltpu.make_async_copy(source, grad.at[target], grad_sems.at[target]).start()
            if fused:
                for target in range(planes):
                    source = sources(target, plane, inner_only)[1]
                    for distance in range(pieces):
                        in_copy(target, distance, source).start()

        per_plane_and_role(start_shards)
        if fused:
            in_copies += [in_copy(t, d, here_refs[1]) for t in range(planes) for d in range(pieces)]
        else:
            in_copies.append(pltpu.make_async_copy(in_refs[0], inner, in_sems.at[0]))
            in_copies[0].start()
        for copy in eig_copies:
            copy.start()
        if second:

            def start_earlier(plane):
                for target in range(planes):
                    source = earlier[relative(target, plane)]
                    pltpu.make_async_copy(source, total.at[target], sum_sems.at[target]).start()

            per_plane(start_earlier)

        for copy in out_copies:
            copy.wait()
        work[...] = jnp.zeros_like(work)

        @pl.loop(0, planes)
        def _(target):
            pltpu.make_async_copy(here_refs[0], grad.at[target], grad_sems.at[target]).wait()
            window = pl.ds(pl.multiple_of(target * rows, rows), rows)
            left = split(cols[window, :])
            cols_high[window, :] = left[0]
            cols_low[window, :] = left[1]
            work[...] += three_pass(left, split(grad[target]), ((0,), (0,)))

        for copy in in_copies:
            copy.wait()
        rotated[...] = three_pass(split(work[...]), split(inner[...]), ((1,), (0,)))
        for copy in eig_copies:
            copy.wait()
        alive = (live > 0).astype(F32)
        turned = rotated[...]
        scaled = turned / (eig[...] + damping_fixed) * alive
        work[...] = scaled
        energy[...] = jnp.sum(turned * scaled, axis=0, keepdims=True)
        high, low = split(three_pass(split(work[...]), split(inner[...]), ((1,), (1,))))
        back_high[...] = high
        back_low[...] = low

        def out_copy(target, plane):
            return pltpu.make_async_copy(
                total.at[target], sums[relative(target, plane)], sum_sems.at[planes + target]
            )

        for target in range(planes):
            window = pl.ds(target * rows, rows)
            product = three_pass(
                (cols_high[window, :], cols_low[window, :]), (back_high[...], back_low[...]), ((1,), (0,))
            )
            if second:
                pltpu.make_async_copy(earlier[0], total.at[target], sum_sems.at[target]).wait()
                total[target] += product
            else:
                total[target] = product
            per_plane(lambda plane, target=target: out_copy(target, plane).start())
        for target in range(planes):
            out_copy(target, target).wait()

    def idle():
        energy[...] = jnp.zeros_like(energy)
        if not second:
            total[0] = jnp.zeros_like(total[0])
            copy = pltpu.make_async_copy(total.at[0], sums[0], sum_sems.at[0])
            copy.start()
            copy.wait()

    least = TWO_BLOCKS if second else ONE_BLOCK
    pl.when(role >= least)(compute)
    pl.when(role < least)(idle)


def run_block(planes, block, inner_job, meta, shards, owns, pieces, inners, earlier=None):
    second = earlier is not None
    rows, width = shards[0].shape
    operands = [*shards, *owns, *pieces, *inners, *(earlier or [])]
    in_hbm = pl.BlockSpec(memory_space=pltpu.HBM)
    sums = [jax.ShapeDtypeStruct((rows, width), F32)] * (2 * planes - 1)
    first_alias = 1 + len(operands) - len(sums)
    number = len(pieces) + (1 if owns else 0)
    dma = pltpu.SemaphoreType.DMA
    flops = 2 * block * width * (2 * rows * planes + 2 * width)
    results = pl.pallas_call(
        functools.partial(block_kernel, planes, inner_job, second, len(owns), len(pieces), not inners),
        out_shape=[*sums, jax.ShapeDtypeStruct((1, width), F32)],
        in_specs=[pl.BlockSpec(memory_space=pltpu.SMEM)] + [in_hbm] * len(operands),
        out_specs=[in_hbm] * len(sums) + [pl.BlockSpec(memory_space=pltpu.VMEM)],
        scratch_shapes=[
            pltpu.VMEM((planes, rows, width), F32),
            pltpu.VMEM((planes * rows, block), F32),
            pltpu.VMEM((planes * rows, block), BF16),
            pltpu.VMEM((planes * rows, block), BF16),
            pltpu.VMEM((block, width), F32),
            pltpu.VMEM((width, width), F32),
            pltpu.VMEM((block, width), F32),
            pltpu.VMEM((block, width), F32),
            pltpu.VMEM((block, width), BF16),
            pltpu.VMEM((block, width), BF16),
            pltpu.VMEM((planes, rows, width), F32),
            dma((number,)),
            dma((1 + number * max(1, width * number // block),)),
            dma((planes,)),
            dma((planes * number,)),
            dma((2 * planes,)),
        ],
        input_output_aliases={first_alias + i: i for i in range(len(sums))} if second else {},
        cost_estimate=pl.CostEstimate(flops=3 * flops, bytes_accessed=4 * 5 * rows * planes * width, transcendentals=0),
        compiler_params=pltpu.CompilerParams(vmem_limit_bytes=56 * 1024 * 1024),
        name="second_block" if second else "first_block",
    )(meta, *operands)
    return results[:-1], results[-1]


def shards(grads, basis_out, basis_in, eigvals, counts, slot_query):
    experts = lax.axis_size("expert")
    planes = lax.axis_size("matrix")
    layers = lax.axis_size("layer")
    expert = lax.axis_index("expert")
    here = lax.axis_index("matrix")
    layer = lax.axis_index("layer")
    rows, width = grads.shape[2], grads.shape[3]
    depth = rows * planes
    last = planes - 1
    inward = [l == 0 and layers == 2 and planes == 4 for l in range(layers)]

    takes_over = jnp.asarray(inward)[layer]
    at_end = (here == 0) | (here == last)
    role = jnp.where(takes_over, jnp.where(at_end, IDLE, TWO_BLOCKS), ONE_BLOCK)
    meta = jnp.stack([here, role, expert, counts[0]]).astype(jnp.int32)

    def move(x, pairs):
        return lax.ppermute(x, ("layer", "matrix"), [(l * planes + a, l * planes + b) for l, a, b in pairs])

    def mirror(pairs):
        return [(l, last - a, last - b) for l, a, b in pairs]

    def gather_pairs(step):
        pairs = [(l, a, a + 1) for l in range(layers) if not inward[l] for a in range(step - 1, last)]
        if step == 1:
            pairs += [(l, a, a + 1) for l in range(layers) if inward[l] for a in range(last - 1)]
        if step == last:
            pairs += [(l, 1, last - 1) for l in range(layers) if inward[l]]
        return pairs

    def reduce_pairs(step):
        low = [1 if inward[l] else 0 for l in range(layers)]
        return [(l, a, a + 1) for l in range(layers) for a in range(low[l], step)]

    def token(x, y):
        mark = x[:8, :128] + y[:8, :128]
        return lax.ppermute(mark, ("layer", "matrix"), [(planes + m, m) for m in range(planes)])

    def gather(x, ties):
        ups, downs = [x], [x]
        for step in range(1, planes):
            up, down = ups[-1], downs[-1]
            before = list(ties.get(step, ()))
            if any(inward) and step == last:
                before.append(token(up, down))
                up = jnp.where(takes_over, ups[1], up)
                down = jnp.where(takes_over, downs[1], down)
            (up, down), _ = lax.optimization_barrier(((up, down), before))
            ups.append(move(up, gather_pairs(step)))
            downs.append(move(down, mirror(gather_pairs(step))))
        return ups[1:], downs[1:]

    columns, heights = basis_out.shape[2], eigvals.shape[1]
    block = experts * columns
    fits = columns % 128 == 0 and width % columns == 0 and columns == heights
    fits = fits and basis_in.shape[1] % 8 == 0 and experts & (experts - 1) == 0

    def crossing(x, distance):
        return lax.ppermute(x, "expert", [(e, e ^ distance) for e in range(experts)])

    end_pairs = [pair for l in range(layers) if inward[l] for pair in ((l, 0, 1), (l, last, last - 1))]
    own = grads[0, 0]
    if fits:
        parts = [
            lax.dynamic_index_in_dim(basis_in, lax.bitwise_xor(expert, distance), 0, keepdims=False)
            for distance in range(experts)
        ]
        parts = [x if d == 0 else crossing(x, d) for d, x in enumerate(parts)]
        packed = pack(meta, basis_out, eigvals)
        parts, packed = lax.optimization_barrier((parts, packed))
        pieces = [crossing(packed[d], d) for d in range(1, experts)]
        over = [move(x, end_pairs) for x in (packed[0], *pieces)] if any(inward) else []
        part, payload = join([parts, [own, *parts]], packed[-1])
        below, above = gather(payload, {2: pieces[:-1], 3: [*pieces[-1:], *over[:2]]})
        here_shards = [own, part]
        first_owns, first_pieces, inners = [basis_out, eigvals], pieces, []
    else:
        eig = lax.all_to_all(eigvals, "expert", split_axis=0, concat_axis=1, tiled=True)[0]
        out = lax.all_to_all(basis_out, "expert", split_axis=0, concat_axis=2, tiled=True)[0]
        inner = lax.all_gather(basis_in, "matrix", axis=1, tiled=True)
        inner = lax.all_to_all(inner, "expert", split_axis=0, concat_axis=0, tiled=True).reshape(width, width)
        below, above = gather(own, {})
        over = []
        here_shards = [own]
        first_owns, first_pieces, inners = [out, eig], [], [inner]

    shards_of_job = [*here_shards, *below, *above]
    sums, energy = run_block(planes, block, any(inward), meta, shards_of_job, first_owns, first_pieces, inners)
    if any(inward):
        owns = [] if fits else [move(x, end_pairs) for x in first_owns]
        sums, more = run_block(planes, block, True, meta, shards_of_job, owns, over, inners, sums)
        energy = energy + more

    value = jnp.sum(energy) / (depth * width)
    scores = jnp.where(jnp.arange(QUERIES, dtype=jnp.int32) == slot_query[0, 0], value, 0.0)
    for axis, size in (("expert", experts), ("matrix", planes)):
        if size & (size - 1):
            scores = lax.psum(scores, axis)
            continue
        distance = 1
        while distance < size:
            turns = [distance * turn for turn in (1, 2, 3) if distance * turn < size]
            moved = [lax.ppermute(scores, axis, [(i, i ^ turn) for i in range(size)]) for turn in turns]
            scores = sum(moved, scores)
            distance *= 4

    below, above = sums[1:planes], sums[planes:]

    def spread(partials, turn):
        moved = None
        for step in range(1, planes):
            partial = partials[last - step]
            sent = partial if moved is None else partial + moved
            moved = move(sent, turn(reduce_pairs(step)))
        return moved

    result = sums[0] + (spread(above, lambda pairs: pairs) + spread(below, mirror))
    return (result[None, None], scores)


def solution(mesh):
    in_specs = (
        P(("layer", "expert"), None, "matrix", None),
        P("layer", None, ("expert", "matrix")),
        P("layer", ("expert", "matrix"), None),
        P("layer", ("expert", "matrix"), None),
        P(("layer", "expert")),
        P(("layer", "expert"), None),
    )
    out_specs = (P(("layer", "expert"), None, "matrix", None), P("layer"))
    return jax.shard_map(shards, mesh=mesh, in_specs=in_specs, out_specs=out_specs, check_vma=False)
```

```python
import functools

import jax
import jax.numpy as jnp
from jax import lax
from jax.experimental import pallas as pl
from jax.experimental.pallas import tpu as pltpu
from jax.sharding import PartitionSpec as P

QUERIES = 32

damping_fixed = 0.05
F32 = jnp.float32
BF16 = jnp.bfloat16

IDLE, ONE_BLOCK, TWO_BLOCKS = 0, 1, 2


def split(x):
    high = x.astype(BF16)
    return high, (x - high.astype(F32)).astype(BF16)


def three_pass(a, b, contract):
    dims = (contract, ((), ()))
    dot = functools.partial(lax.dot_general, dimension_numbers=dims, preferred_element_type=F32)
    return dot(a[0], b[0]) + (dot(a[0], b[1]) + dot(a[1], b[0]))


def pack_kernel(experts, meta, outs, eigs, *refs):
    packed, tail, sems = refs[:experts], refs[experts], refs[experts + 1]
    depth, width = outs.shape[1], outs.shape[2]
    height = eigs.shape[1]
    chunks = eigs.shape[2] // width
    copies = []
    for distance in range(experts):
        target = lax.bitwise_xor(meta[2], distance)
        base = distance * (chunks + 1)
        into, start = packed[distance], depth
        first = min(depth, into.shape[0])
        copies.append(
            pltpu.make_async_copy(
                outs.at[target, pl.ds(0, first), :], into.at[pl.ds(0, first), :], sems.at[base]
            )
        )
        if first < depth:
            into, start = tail, depth - first
            copies.append(
                pltpu.make_async_copy(
                    outs.at[target, pl.ds(first, start), :], into.at[pl.ds(0, start), :], sems.at[base + chunks + 1]
                )
            )
        for chunk in range(chunks):
            copies.append(
                pltpu.make_async_copy(
                    eigs.at[target, :, pl.ds(chunk * width, width)],
                    into.at[pl.ds(start + chunk * height, height), :],
                    sems.at[base + 1 + chunk],
                )
            )
    for copy in copies:
        copy.start()
    for copy in copies:
        copy.wait()


def pack(meta, outs, eigs):
    experts, depth, width = outs.shape
    chunks = eigs.shape[2] // width
    in_hbm = pl.BlockSpec(memory_space=pltpu.HBM)
    shape = jax.ShapeDtypeStruct((depth + chunks * eigs.shape[1], width), F32)
    half = jax.ShapeDtypeStruct((shape.shape[0] // 2, width), F32)
    return pl.pallas_call(
        functools.partial(pack_kernel, experts),
        out_shape=[shape] * (experts - 1) + [half] * 2,
        in_specs=[pl.BlockSpec(memory_space=pltpu.SMEM), in_hbm, in_hbm],
        out_specs=[pl.BlockSpec(memory_space=pltpu.VMEM)] * (experts + 1),
        scratch_shapes=[pltpu.SemaphoreType.DMA((experts * (chunks + 1) + 1,))],
        compiler_params=pltpu.CompilerParams(vmem_limit_bytes=32 * 1024 * 1024),
        cost_estimate=pl.CostEstimate(flops=0, bytes_accessed=8 * (outs.size + eigs.size), transcendentals=0),
        name="pack",
    )(meta, outs, eigs)


def join_kernel(refs_in, groups, *refs):
    sources, outs, sems = refs[1 : 1 + refs_in], refs[1 + refs_in : -1], refs[-1]
    copies = []
    at = 0
    for out, number in zip(outs, groups):
        first = 0
        for source in sources[at : at + number]:
            height = source.shape[0]
            copies.append(pltpu.make_async_copy(source, out.at[pl.ds(first, height), :], sems.at[len(copies)]))
            first += height
        at += number
    for copy in copies:
        copy.start()
    for copy in copies:
        copy.wait()


def join(groups, after):
    sources = [x for group in groups for x in group]
    in_hbm = pl.BlockSpec(memory_space=pltpu.HBM)
    shapes = [jax.ShapeDtypeStruct((sum(x.shape[0] for x in group), group[0].shape[1]), F32) for group in groups]
    return pl.pallas_call(
        functools.partial(join_kernel, len(sources), [len(group) for group in groups]),
        out_shape=shapes,
        in_specs=[in_hbm] * (1 + len(sources)),
        out_specs=[pl.BlockSpec(memory_space=pltpu.VMEM)] * len(shapes),
        scratch_shapes=[pltpu.SemaphoreType.DMA((len(sources),))],
        cost_estimate=pl.CostEstimate(flops=0, bytes_accessed=8 * sum(x.size for x in sources), transcendentals=0),
        compiler_params=pltpu.CompilerParams(vmem_limit_bytes=32 * 1024 * 1024),
        name="join",
    )(after, *sources)


def block_kernel(planes, inner_job, second, n_own, n_piece, fused, meta, *refs):
    refs = list(refs)

    def take(number):
        taken, refs[:number] = refs[:number], []
        return taken

    hops = planes - 1
    here_refs = take(2 if fused else 1)
    up_refs, down_refs = take(hops), take(hops)
    own_refs, piece_refs = take(n_own), take(n_piece)
    tail_refs = take(1 if n_piece else 0)
    in_refs = take(0 if fused else 1)
    earlier = take(2 * planes - 1) if second else None
    sums = take(2 * planes - 1)
    (energy,) = take(1)
    grad, cols, cols_high, cols_low, eig, inner, work, rotated, back_high, back_low, total = take(11)
    out_sems, eig_sems, grad_sems, in_sems, sum_sems = refs
    rows = grad.shape[1]
    here, role, expert, live = meta[0], meta[1], meta[2], meta[3]
    depth, block = cols.shape

    def relative(target, plane):
        if target < plane:
            return plane - target
        if target > plane:
            return hops + target - plane
        return 0

    def per_plane(action):
        for plane in range(planes):
            pl.when(here == plane)(functools.partial(action, plane))

    def per_plane_and_role(action):
        if not second:
            for plane in range(planes):
                pl.when((here == plane) & (role == ONE_BLOCK))(functools.partial(action, plane, False))
        if inner_job:
            for plane in (1, planes - 2):
                pl.when((here == plane) & (role == TWO_BLOCKS))(functools.partial(action, plane, True))

    def sources(target, plane, inner_only):
        distance = abs(target - plane)
        if distance == 0:
            return here_refs
        step = hops if inner_only and distance > 1 else distance
        ref = (up_refs if target < plane else down_refs)[step - 1]
        if not fused:
            return [ref]
        return [ref.at[pl.ds(0, rows), :], ref.at[pl.ds(rows, ref.shape[0] - rows), :]]

    def compute():
        pieces = n_piece + (1 if n_own else 0)
        width = height = block // pieces
        out_copies, eig_copies = [], []

        def place(copies, sems, source, spot):
            copies.append(pltpu.make_async_copy(source, spot, sems.at[len(copies)]))

        owns = [ref.at[expert] if len(ref.shape) == 3 else ref for ref in own_refs]
        first = 1 if n_own else 0
        if n_own:
            place(out_copies, out_sems, owns[0], cols.at[:, pl.ds(0, width)])
            place(eig_copies, eig_sems, owns[1], eig.at[pl.ds(0, height), :])
        for index, ref in enumerate(piece_refs, first):
            top, start = min(depth, ref.shape[0]), depth
            slot = pl.ds(index * width, width)
            place(out_copies, out_sems, ref.at[pl.ds(0, top), :], cols.at[pl.ds(0, top), slot])
            if top < depth:
                ref, start = tail_refs[0], depth - top
                place(out_copies, out_sems, ref.at[pl.ds(0, start), :], cols.at[pl.ds(top, start), slot])
            for chunk in range(eig.shape[1] // width):
                spot = eig.at[pl.ds(index * height, height), pl.ds(chunk * width, width)]
                place(eig_copies, eig_sems, ref.at[pl.ds(start + chunk * height, height), :], spot)
        for copy in out_copies:
            copy.start()

        in_copies = []

        def in_copy(target, distance, source):
            part = source.shape[0] // pieces
            owner = lax.bitwise_xor(expert, distance)
            to = pl.multiple_of((owner * planes + target) * part, part)
            window = source.at[pl.ds(distance * part, part), :]
            sem = in_sems.at[target * pieces + distance]
            return pltpu.make_async_copy(window, inner.at[pl.ds(to, part), :], sem)

        def start_shards(plane, inner_only):
            for target in range(planes):
                source = sources(target, plane, inner_only)[0]
                pltpu.make_async_copy(source, grad.at[target], grad_sems.at[target]).start()
            if fused:
                for target in range(planes):
                    source = sources(target, plane, inner_only)[1]
                    for distance in range(pieces):
                        in_copy(target, distance, source).start()

        per_plane_and_role(start_shards)
        if fused:
            in_copies += [in_copy(t, d, here_refs[1]) for t in range(planes) for d in range(pieces)]
        else:
            in_copies.append(pltpu.make_async_copy(in_refs[0], inner, in_sems.at[0]))
            in_copies[0].start()
        for copy in eig_copies:
            copy.start()
        if second:

            def start_earlier(plane):
                for target in range(planes):
                    source = earlier[relative(target, plane)]
                    pltpu.make_async_copy(source, total.at[target], sum_sems.at[target]).start()

            per_plane(start_earlier)

        for copy in out_copies:
            copy.wait()
        work[...] = jnp.zeros_like(work)

        @pl.loop(0, planes)
        def _(target):
            pltpu.make_async_copy(here_refs[0], grad.at[target], grad_sems.at[target]).wait()
            window = pl.ds(pl.multiple_of(target * rows, rows), rows)
            left = split(cols[window, :])
            cols_high[window, :] = left[0]
            cols_low[window, :] = left[1]
            work[...] += three_pass(left, split(grad[target]), ((0,), (0,)))

        for copy in in_copies:
            copy.wait()
        rotated[...] = three_pass(split(work[...]), split(inner[...]), ((1,), (0,)))
        for copy in eig_copies:
            copy.wait()
        alive = (live > 0).astype(F32)
        turned = rotated[...]
        scaled = turned / (eig[...] + damping_fixed) * alive
        work[...] = scaled
        energy[...] = jnp.sum(turned * scaled, axis=0, keepdims=True)
        high, low = split(three_pass(split(work[...]), split(inner[...]), ((1,), (1,))))
        back_high[...] = high
        back_low[...] = low

        def out_copy(target, plane):
            return pltpu.make_async_copy(
                total.at[target], sums[relative(target, plane)], sum_sems.at[planes + target]
            )

        for target in range(planes):
            window = pl.ds(target * rows, rows)
            product = three_pass(
                (cols_high[window, :], cols_low[window, :]), (back_high[...], back_low[...]), ((1,), (0,))
            )
            if second:
                pltpu.make_async_copy(earlier[0], total.at[target], sum_sems.at[target]).wait()
                total[target] += product
            else:
                total[target] = product
            per_plane(lambda plane, target=target: out_copy(target, plane).start())
        for target in range(planes):
            out_copy(target, target).wait()

    def idle():
        energy[...] = jnp.zeros_like(energy)
        if not second:
            total[0] = jnp.zeros_like(total[0])
            copy = pltpu.make_async_copy(total.at[0], sums[0], sum_sems.at[0])
            copy.start()
            copy.wait()

    least = TWO_BLOCKS if second else ONE_BLOCK
    pl.when(role >= least)(compute)
    pl.when(role < least)(idle)


def run_block(planes, block, inner_job, meta, shards, owns, pieces, inners, earlier=None):
    second = earlier is not None
    rows, width = shards[0].shape
    operands = [*shards, *owns, *pieces, *inners, *(earlier or [])]
    in_hbm = pl.BlockSpec(memory_space=pltpu.HBM)
    sums = [jax.ShapeDtypeStruct((rows, width), F32)] * (2 * planes - 1)
    first_alias = 1 + len(operands) - len(sums)
    n_piece = max(0, len(pieces) - 1)
    number = n_piece + (1 if owns else 0)
    dma = pltpu.SemaphoreType.DMA
    flops = 2 * block * width * (2 * rows * planes + 2 * width)
    results = pl.pallas_call(
        functools.partial(block_kernel, planes, inner_job, second, len(owns), n_piece, not inners),
        out_shape=[*sums, jax.ShapeDtypeStruct((1, width), F32)],
        in_specs=[pl.BlockSpec(memory_space=pltpu.SMEM)] + [in_hbm] * len(operands),
        out_specs=[in_hbm] * len(sums) + [pl.BlockSpec(memory_space=pltpu.VMEM)],
        scratch_shapes=[
            pltpu.VMEM((planes, rows, width), F32),
            pltpu.VMEM((planes * rows, block), F32),
            pltpu.VMEM((planes * rows, block), BF16),
            pltpu.VMEM((planes * rows, block), BF16),
            pltpu.VMEM((block, width), F32),
            pltpu.VMEM((width, width), F32),
            pltpu.VMEM((block, width), F32),
            pltpu.VMEM((block, width), F32),
            pltpu.VMEM((block, width), BF16),
            pltpu.VMEM((block, width), BF16),
            pltpu.VMEM((planes, rows, width), F32),
            dma((number + 1,)),
            dma((1 + number * max(1, width * number // block),)),
            dma((planes,)),
            dma((planes * number,)),
            dma((2 * planes,)),
        ],
        input_output_aliases={first_alias + i: i for i in range(len(sums))} if second else {},
        cost_estimate=pl.CostEstimate(flops=3 * flops, bytes_accessed=4 * 5 * rows * planes * width, transcendentals=0),
        compiler_params=pltpu.CompilerParams(vmem_limit_bytes=56 * 1024 * 1024),
        name="second_block" if second else "first_block",
    )(meta, *operands)
    return results[:-1], results[-1]


def shards(grads, basis_out, basis_in, eigvals, counts, slot_query):
    experts = lax.axis_size("expert")
    planes = lax.axis_size("matrix")
    layers = lax.axis_size("layer")
    expert = lax.axis_index("expert")
    here = lax.axis_index("matrix")
    layer = lax.axis_index("layer")
    rows, width = grads.shape[2], grads.shape[3]
    depth = rows * planes
    last = planes - 1
    inward = [l == 0 and layers == 2 and planes == 4 for l in range(layers)]

    takes_over = jnp.asarray(inward)[layer]
    at_end = (here == 0) | (here == last)
    role = jnp.where(takes_over, jnp.where(at_end, IDLE, TWO_BLOCKS), ONE_BLOCK)
    meta = jnp.stack([here, role, expert, counts[0]]).astype(jnp.int32)

    def move(x, pairs):
        return lax.ppermute(x, ("layer", "matrix"), [(l * planes + a, l * planes + b) for l, a, b in pairs])

    def mirror(pairs):
        return [(l, last - a, last - b) for l, a, b in pairs]

    def gather_pairs(step):
        pairs = [(l, a, a + 1) for l in range(layers) if not inward[l] for a in range(step - 1, last)]
        if step == 1:
            pairs += [(l, a, a + 1) for l in range(layers) if inward[l] for a in range(last - 1)]
        if step == last:
            pairs += [(l, 1, last - 1) for l in range(layers) if inward[l]]
        return pairs

    def reduce_pairs(step):
        low = [1 if inward[l] else 0 for l in range(layers)]
        return [(l, a, a + 1) for l in range(layers) for a in range(low[l], step)]

    def token(x, y):
        mark = x[:8, :128] + y[:8, :128]
        return lax.ppermute(mark, ("layer", "matrix"), [(planes + m, m) for m in range(planes)])

    def gather(x, ties):
        ups, downs = [x], [x]
        for step in range(1, planes):
            up, down = ups[-1], downs[-1]
            before = list(ties.get(step, ()))
            if any(inward) and step == last:
                before.append(token(up, down))
                up = jnp.where(takes_over, ups[1], up)
                down = jnp.where(takes_over, downs[1], down)
            (up, down), _ = lax.optimization_barrier(((up, down), before))
            ups.append(move(up, gather_pairs(step)))
            downs.append(move(down, mirror(gather_pairs(step))))
        return ups[1:], downs[1:]

    columns, heights = basis_out.shape[2], eigvals.shape[1]
    block = experts * columns
    fits = columns % 128 == 0 and width % columns == 0 and columns == heights
    fits = fits and basis_in.shape[1] % 8 == 0 and experts & (experts - 1) == 0

    def crossing(x, distance):
        return lax.ppermute(x, "expert", [(e, e ^ distance) for e in range(experts)])

    end_pairs = [pair for l in range(layers) if inward[l] for pair in ((l, 0, 1), (l, last, last - 1))]
    own = grads[0, 0]
    if fits:
        parts = [
            lax.dynamic_index_in_dim(basis_in, lax.bitwise_xor(expert, distance), 0, keepdims=False)
            for distance in range(experts)
        ]
        parts = [x if d == 0 else crossing(x, d) for d, x in enumerate(parts)]
        packed = pack(meta, basis_out, eigvals)
        parts, packed = lax.optimization_barrier((parts, packed))
        pieces = [crossing(x, min(d, experts - 1)) for d, x in enumerate(packed) if d]
        over = [move(x, end_pairs) for x in (packed[0], *pieces)] if any(inward) else []
        part, payload = join([parts, [own, *parts]], packed[-1])
        below, above = gather(payload, {2: pieces[:-1], 3: [*pieces[-1:], *over[:1]]})
        here_shards = [own, part]
        first_owns, first_pieces, inners = [basis_out, eigvals], pieces, []
    else:
        eig = lax.all_to_all(eigvals, "expert", split_axis=0, concat_axis=1, tiled=True)[0]
        out = lax.all_to_all(basis_out, "expert", split_axis=0, concat_axis=2, tiled=True)[0]
        inner = lax.all_gather(basis_in, "matrix", axis=1, tiled=True)
        inner = lax.all_to_all(inner, "expert", split_axis=0, concat_axis=0, tiled=True).reshape(width, width)
        below, above = gather(own, {})
        over = []
        here_shards = [own]
        first_owns, first_pieces, inners = [out, eig], [], [inner]

    shards_of_job = [*here_shards, *below, *above]
    sums, energy = run_block(planes, block, any(inward), meta, shards_of_job, first_owns, first_pieces, inners)
    if any(inward):
        owns = [] if fits else [move(x, end_pairs) for x in first_owns]
        sums, more = run_block(planes, block, True, meta, shards_of_job, owns, over, inners, sums)
        energy = energy + more

    value = jnp.sum(energy) / (depth * width)
    scores = jnp.where(jnp.arange(QUERIES, dtype=jnp.int32) == slot_query[0, 0], value, 0.0)
    for axis, size in (("expert", experts), ("matrix", planes)):
        if size & (size - 1):
            scores = lax.psum(scores, axis)
            continue
        distance = 1
        while distance < size:
            turns = [distance * turn for turn in (1, 2, 3) if distance * turn < size]
            moved = [lax.ppermute(scores, axis, [(i, i ^ turn) for i in range(size)]) for turn in turns]
            scores = sum(moved, scores)
            distance *= 4

    below, above = sums[1:planes], sums[planes:]

    def spread(partials, turn):
        moved = None
        for step in range(1, planes):
            partial = partials[last - step]
            sent = partial if moved is None else partial + moved
            moved = move(sent, turn(reduce_pairs(step)))
        return moved

    result = sums[0] + (spread(above, lambda pairs: pairs) + spread(below, mirror))
    return (result[None, None], scores)


def solution(mesh):
    in_specs = (
        P(("layer", "expert"), None, "matrix", None),
        P("layer", None, ("expert", "matrix")),
        P("layer", ("expert", "matrix"), None),
        P("layer", ("expert", "matrix"), None),
        P(("layer", "expert")),
        P(("layer", "expert"), None),
    )
    out_specs = (P(("layer", "expert"), None, "matrix", None), P("layer"))
    return jax.shard_map(shards, mesh=mesh, in_specs=in_specs, out_specs=out_specs, check_vma=False)
```
